32 devices in a mesh: section: 2 (over x), expert: 16 (over z, y, core).
Axes of the slice: x: 2, y: 2, z: 4, core: 2. Of those that a mesh axis runs over, the one named last changes fastest.
Arguments:
- fwd_act: bfloat16 [2, 1024, 3584], P('section', 'expert'), may hold values from -6 to 6
- fwd_route: int32 [2, 1024], P('section', 'expert'), may hold values from 0 to 3, as said below
- fwd_weight: float32 [2, 1024], P('section', 'expert'), may hold values from 0.5 to 2.5
- bwd_act: bfloat16 [2, 1024, 3584], P('section', 'expert'), may hold values from -6 to 6
- bwd_grad: bfloat16 [2, 1024, 3584], P('section', 'expert'), may hold values from -6 to 6
- bwd_route: int32 [2, 1024], P('section', 'expert'), may hold values from 0 to 3, as said below
- bwd_weight: float32 [2, 1024], P('section', 'expert'), may hold values from 0.5 to 2.5
- w_gate: bfloat16 [2, 3584, 2048], P('section', None, 'expert'), may hold values from -0.09375 to 0.09375
- w_up: bfloat16 [2, 3584, 2048], P('section', None, 'expert'), may hold values from -0.09375 to 0.09375
- w_down: bfloat16 [2, 2048, 3584], P('section', 'expert'), may hold values from -0.1875 to 0.1875
Outputs:
- mixed: bfloat16 [2, 1024, 3584], P('section', 'expert')
- input_grad: bfloat16 [2, 1024, 3584], P('section', 'expert')
- gate_grad: float32 [2, 1024], P('section', 'expert')
The draws below stay inside these ranges and needn't reach their ends.
Inputs may be any that keep to these rules, and one draw needn't show every extreme that they name: `fwd_route`: in the 64 tokens of one device no id occurs more than 24 times; in each section one id below 2 occurs exactly 24 times in the tokens of every device of that section. `bwd_route`: as for fwd_route.
All inputs are finite; a program needn't handle non-finite values.
Results may differ from the reference program's by a relative error of at most 0.0095.
Values may be sent and summed in bfloat16 or wider, within the bound.
A program may use at most 64 MiB of HBM per device.

```python
import jax
import jax.numpy as jnp
from jax import lax

D = 3584
FF = 1024
FF_DEV = 128
TOK_MB = 64
GROUP = 8
EXPERTS = 2
ROUTED = 4
CAP = 24
ROWS = 384
TOKENS = 1024
N_SECTION = 2
N_EXPERT = 16


def route_law(key):
    slots = ROUTED * CAP
    blocks = N_SECTION * N_EXPERT
    owner = jnp.arange(slots, dtype=jnp.int32) // CAP
    index = jnp.arange(slots, dtype=jnp.int32)
    key_hot, key_pop, key_noise, key_perm = jax.random.split(key, 4)
    hot = jax.random.randint(key_hot, (N_SECTION,), 0, EXPERTS)
    favour = jax.random.randint(key_pop, (N_SECTION, ROUTED), 0, 4)
    hot_rows = jnp.repeat(hot, N_EXPERT)
    favour_rows = jnp.repeat(favour, N_EXPERT, axis=0)
    noise = jax.random.randint(key_noise, (blocks, slots), 0, 4096)
    score = (jnp.take(favour_rows, owner, axis=1) * 4096 + noise) * slots + index[None, :]
    score = jnp.where(owner[None, :] == hot_rows[:, None], 2 ** 30 + index[None, :], score)
    order = jnp.argsort(-score, axis=1)
    chosen = jnp.take(owner, order[:, :TOK_MB])
    mixing = jax.random.randint(key_perm, (blocks, TOK_MB), 0, 2 ** 20) * TOK_MB + jnp.arange(TOK_MB, dtype=jnp.int32)[None, :]
    shuffle = jnp.argsort(mixing, axis=1)
    routes = jnp.take_along_axis(chosen, shuffle, axis=1)
    return routes.reshape(N_SECTION, N_EXPERT * TOK_MB).astype(jnp.int32)


def draw_fwd_route(key, part):
    key = jax.random.fold_in(key, 11)
    return route_law(key)


def draw_bwd_route(key, part):
    key = jax.random.fold_in(key, 12)
    return route_law(key)


def block_scale(key, extent, cuts, smallest, largest):
    gain = 1.0
    for axis_at, shards_of in cuts:
        steps = jax.random.uniform(jax.random.fold_in(jax.random.fold_in(key, 6), axis_at), (shards_of,), jnp.float32, smallest / len(cuts), largest / len(cuts))
        gain = gain * jnp.repeat(jnp.exp(steps), extent[axis_at] // shards_of).reshape((-1,) + (1,) * (len(extent) - 1 - axis_at))
    return gain


def normal_values(own_key, extent, deviation, limit, cuts=(), kind=jnp.bfloat16):
    gain = block_scale(own_key, extent, cuts, -0.22, 0.18) if cuts else 1.0
    entries = jax.random.normal(own_key, extent, jnp.float32) * deviation * gain
    return jnp.minimum(jnp.maximum(entries, -limit), limit).astype(kind)


def setup_inputs(seed: int = 0) -> dict:
    streams_of = jax.random.split(jax.random.key(seed), 11)
    fwd_act = normal_values(streams_of[0], (N_SECTION, TOKENS, D), 1.0, 6.0, ((0, 2), (1, 16)))
    fwd_route = draw_fwd_route(jax.random.fold_in(streams_of[10], 71), 0)
    fwd_weight = jnp.clip(0.5 + 2.0 * jax.random.uniform(streams_of[2], (N_SECTION, TOKENS), jnp.float32) ** block_scale(streams_of[2], (N_SECTION, TOKENS), ((0, 2), (1, 16)), -0.2, 0.2), 0.5, 2.5)
    bwd_act = normal_values(streams_of[3], (N_SECTION, TOKENS, D), 1.0, 6.0, ((0, 2), (1, 16)))
    bwd_grad = normal_values(streams_of[4], (N_SECTION, TOKENS, D), 1.0, 6.0, ((0, 2), (1, 16)))
    bwd_route = draw_bwd_route(jax.random.fold_in(streams_of[10], 71), 0)
    bwd_weight = jnp.clip(0.5 + 2.0 * jax.random.uniform(streams_of[6], (N_SECTION, TOKENS), jnp.float32) ** block_scale(streams_of[6], (N_SECTION, TOKENS), ((0, 2), (1, 16)), -0.2, 0.2), 0.5, 2.5)
    w_gate = normal_values(streams_of[7], (N_SECTION, D, EXPERTS * FF), D ** -0.5, 0.09375, ((0, 2), (2, 16)))
    w_up = normal_values(streams_of[8], (N_SECTION, D, EXPERTS * FF), D ** -0.5, 0.09375, ((0, 2), (2, 16)))
    w_down = normal_values(streams_of[9], (N_SECTION, EXPERTS * FF, D), FF ** -0.5, 0.1875, ((0, 2), (1, 16)))
    return {"fwd_act": fwd_act, "fwd_route": fwd_route, "fwd_weight": fwd_weight, "bwd_act": bwd_act, "bwd_grad": bwd_grad, "bwd_route": bwd_route, "bwd_weight": bwd_weight, "w_gate": w_gate, "w_up": w_up, "w_down": w_down}


def forward_rows(token_rows, gate_cols, up_cols, down_rows):
    gate_pre = jnp.dot(token_rows, gate_cols, preferred_element_type=jnp.float32)
    up_pre = jnp.dot(token_rows, up_cols, preferred_element_type=jnp.float32)
    hidden = (jax.nn.silu(gate_pre) * up_pre).astype(jnp.bfloat16)
    hidden_slices = hidden.astype(jnp.float32).reshape(hidden.shape[0], GROUP, FF_DEV)
    down_slices = down_rows.astype(jnp.float32).reshape(GROUP, FF_DEV, D)
    partial_value = jnp.einsum('rgh,ghd->rgd', hidden_slices, down_slices).astype(jnp.bfloat16)
    return jnp.sum(partial_value.astype(jnp.float32), axis=1)


def backward_rows(token_rows, grad_rows, gate_cols, up_cols, down_rows):
    gate_pre = jnp.dot(token_rows, gate_cols, preferred_element_type=jnp.float32)
    up_pre = jnp.dot(token_rows, up_cols, preferred_element_type=jnp.float32)
    gate_sig = jax.nn.sigmoid(gate_pre)
    active = gate_pre * gate_sig
    hidden = (active * up_pre).astype(jnp.bfloat16)
    d_hidden = jnp.dot(grad_rows, down_rows.T, preferred_element_type=jnp.float32)
    d_gate = (d_hidden * up_pre * gate_sig * (1.0 + gate_pre * (1.0 - gate_sig))).astype(jnp.bfloat16)
    d_up = (d_hidden * active).astype(jnp.bfloat16)
    count = token_rows.shape[0]
    gate_slices = gate_cols.astype(jnp.float32).reshape(D, GROUP, FF_DEV)
    up_slices = up_cols.astype(jnp.float32).reshape(D, GROUP, FF_DEV)
    d_gate_slices = d_gate.astype(jnp.float32).reshape(count, GROUP, FF_DEV)
    d_up_slices = d_up.astype(jnp.float32).reshape(count, GROUP, FF_DEV)
    partial_value = jnp.einsum('rgh,dgh->rgd', d_gate_slices, gate_slices) + jnp.einsum('rgh,dgh->rgd', d_up_slices, up_slices)
    d_rows = jnp.sum(partial_value.astype(jnp.bfloat16).astype(jnp.float32), axis=1)
    terms = jnp.sum((hidden.astype(jnp.float32) * d_hidden).reshape(count, GROUP, FF_DEV), axis=2).astype(jnp.bfloat16)
    return d_rows, jnp.sum(terms.astype(jnp.float32), axis=1)


def section_pass(items):
    layer_in, route_f, weight_f, act_b, grad_in, route_b, weight_b, gate_w, up_w, down_w = items
    gate_e = gate_w.reshape(D, EXPERTS, FF).transpose(1, 0, 2)
    up_e = up_w.reshape(D, EXPERTS, FF).transpose(1, 0, 2)
    down_e = down_w.reshape(EXPERTS, FF, D)
    blank = jnp.zeros((1, D), jnp.bfloat16)
    pad_f = jnp.concatenate([layer_in, blank], axis=0)
    pad_x = jnp.concatenate([act_b, blank], axis=0)
    pad_g = jnp.concatenate([grad_in, blank], axis=0)

    def per_expert(carry, expert_items):
        acc_f, acc_x, acc_w = carry
        expert, gate_cols, up_cols, down_rows = expert_items
        index_f = jnp.nonzero(route_f == expert, size=ROWS, fill_value=TOKENS)[0].astype(jnp.int32)
        index_b = jnp.nonzero(route_b == expert, size=ROWS, fill_value=TOKENS)[0].astype(jnp.int32)
        out_f = forward_rows(pad_f[index_f], gate_cols, up_cols, down_rows)
        out_x, out_w = backward_rows(pad_x[index_b], pad_g[index_b], gate_cols, up_cols, down_rows)
        return (acc_f.at[index_f].add(out_f), acc_x.at[index_b].add(out_x), acc_w.at[index_b].add(out_w)), None

    start = (jnp.zeros((TOKENS + 1, D), jnp.float32), jnp.zeros((TOKENS + 1, D), jnp.float32), jnp.zeros((TOKENS + 1,), jnp.float32))
    totals, unused = lax.scan(per_expert, start, (jnp.arange(EXPERTS, dtype=jnp.int32), gate_e, up_e, down_e))
    acc_f, acc_x, acc_w = totals
    mixed = (layer_in.astype(jnp.float32) + weight_f[:, None] * acc_f[:TOKENS]).astype(jnp.bfloat16)
    input_grad = (grad_in.astype(jnp.float32) + weight_b[:, None] * acc_x[:TOKENS]).astype(jnp.bfloat16)
    return mixed, input_grad, acc_w[:TOKENS]


def reference(fwd_act, fwd_route, fwd_weight, bwd_act, bwd_grad, bwd_route, bwd_weight, w_gate, w_up, w_down):
    layer_in = jnp.roll(fwd_act, 1, axis=0)
    grad_in = jnp.roll(bwd_grad, -1, axis=0)
    mixed, input_grad, gate_grad = lax.map(section_pass, (layer_in, fwd_route, fwd_weight, bwd_act, grad_in, bwd_route, bwd_weight, w_gate, w_up, w_down))
    return (mixed, input_grad, gate_grad)
```

```python
import functools

import jax
import jax.numpy as jnp
from jax import lax
from jax.experimental import pallas as pl
from jax.experimental.pallas import tpu as pltpu
from jax.sharding import PartitionSpec as P

FF = 1024


def passed_along(block, axis, distance):
    devices = range(lax.axis_size(axis))
    route = [((i - distance) % len(devices), i) for i in devices]
    return lax.ppermute(block, axis, route)


def route_plan(route_ids, experts, capacity):
    route_range = jnp.arange(2 * experts, dtype=jnp.int32)
    onehot = (route_ids[:, None] == route_range[None, :]).astype(jnp.int32)
    before = jnp.cumsum(onehot, axis=0) - onehot
    slot_ids = jnp.sum(before * onehot, axis=1)
    inside = route_ids < experts
    expert_ids = jnp.arange(experts, dtype=jnp.int32)
    slot_range = jnp.arange(capacity, dtype=jnp.int32)
    select = (
        (route_ids[None, None, :] == expert_ids[:, None, None])
        & (slot_ids[None, None, :] == slot_range[None, :, None])
    ).astype(jnp.bfloat16)
    place_at = jnp.where(inside, route_ids * capacity + slot_ids, 0)
    return (select, place_at, inside)


def pack_rows(select, token_rows, group_size):
    packed = jnp.einsum(
        "ect,td->ecd", select, token_rows, preferred_element_type=jnp.float32
    ).astype(jnp.bfloat16)
    copies = jnp.broadcast_to(packed[:, None], (packed.shape[0], group_size) + packed.shape[1:])
    return copies.reshape((packed.shape[0] * group_size,) + packed.shape[1:])


def unpack_sum(returned, group_size, place_at, inside):
    grouped = returned.astype(jnp.float32).reshape(
        (returned.shape[0] // group_size, group_size) + returned.shape[1:]
    )
    summed = jnp.sum(grouped, axis=1)
    flat = summed.reshape((summed.shape[0] * summed.shape[1],) + summed.shape[2:])
    picked = flat[place_at]
    mask = inside.reshape(inside.shape + (1,) * (picked.ndim - 1))
    return jnp.where(mask, picked, 0.0)


def expert_forward(token_rows, gate_cols, up_cols, down_rows):
    gate_pre = jnp.einsum("scd,dh->sch", token_rows, gate_cols, preferred_element_type=jnp.float32)
    up_pre = jnp.einsum("scd,dh->sch", token_rows, up_cols, preferred_element_type=jnp.float32)
    hidden = (jax.nn.silu(gate_pre) * up_pre).astype(jnp.bfloat16)
    return jnp.einsum("sch,hd->scd", hidden, down_rows, preferred_element_type=jnp.float32).astype(
        jnp.bfloat16
    )


def expert_backward(token_rows, grad_rows, gate_cols, up_cols, down_rows):
    gate_pre = jnp.einsum("scd,dh->sch", token_rows, gate_cols, preferred_element_type=jnp.float32)
    up_pre = jnp.einsum("scd,dh->sch", token_rows, up_cols, preferred_element_type=jnp.float32)
    gate_sig = jax.nn.sigmoid(gate_pre)
    active = gate_pre * gate_sig
    hidden = (active * up_pre).astype(jnp.bfloat16)
    d_hidden = jnp.einsum("scd,hd->sch", grad_rows, down_rows, preferred_element_type=jnp.float32)
    d_gate = (d_hidden * up_pre * gate_sig * (1.0 + gate_pre * (1.0 - gate_sig))).astype(
        jnp.bfloat16
    )
    d_up = (d_hidden * active).astype(jnp.bfloat16)
    d_rows = jnp.einsum("sch,dh->scd", d_gate, gate_cols, preferred_element_type=jnp.float32)
    d_rows = (
        d_rows + jnp.einsum("sch,dh->scd", d_up, up_cols, preferred_element_type=jnp.float32)
    ).astype(jnp.bfloat16)
    terms = jnp.sum(hidden.astype(jnp.float32) * d_hidden, axis=2).astype(jnp.bfloat16)
    return (d_rows, terms)


def local(
    fwd_act, fwd_route, fwd_weight, bwd_act, bwd_grad, bwd_route, bwd_weight, w_gate, w_up, w_down
):
    layer_in = passed_along(fwd_act, "section", 1)[0]
    grad_in = passed_along(bwd_grad, "section", -1)[0]
    gate_cols = w_gate[0]
    up_cols = w_up[0]
    down_rows = w_down[0]
    group_size = FF // gate_cols.shape[1]
    experts = lax.axis_size("expert") // group_size
    tok_count = layer_in.shape[0]
    capacity = 3 * tok_count // (4 * experts)
    select_f, place_f, inside_f = route_plan(fwd_route[0], experts, capacity)
    select_b, place_b, inside_b = route_plan(bwd_route[0], experts, capacity)
    sent_f = pack_rows(select_f, layer_in, group_size)
    sent_x = pack_rows(select_b, bwd_act[0], group_size)
    sent_g = pack_rows(select_b, grad_in, group_size)
    part_out = expert_forward(
        lax.all_to_all(sent_f, "expert", split_axis=0, concat_axis=0, tiled=True),
        gate_cols,
        up_cols,
        down_rows,
    )
    back_f = lax.all_to_all(part_out, "expert", split_axis=0, concat_axis=0, tiled=True)
    d_rows, terms = expert_backward(
        lax.all_to_all(sent_x, "expert", split_axis=0, concat_axis=0, tiled=True),
        lax.all_to_all(sent_g, "expert", split_axis=0, concat_axis=0, tiled=True),
        gate_cols,
        up_cols,
        down_rows,
    )
    back_x = lax.all_to_all(d_rows, "expert", split_axis=0, concat_axis=0, tiled=True)
    back_w = lax.all_to_all(terms, "expert", split_axis=0, concat_axis=0, tiled=True)
    total_f = unpack_sum(back_f, group_size, place_f, inside_f)
    total_x = unpack_sum(back_x, group_size, place_b, inside_b)
    gate_grad = unpack_sum(back_w, group_size, place_b, inside_b)
    mixed = (layer_in.astype(jnp.float32) + fwd_weight[0][:, None] * total_f).astype(jnp.bfloat16)
    input_grad = (grad_in.astype(jnp.float32) + bwd_weight[0][:, None] * total_x).astype(
        jnp.bfloat16
    )
    return (mixed[None], input_grad[None], gate_grad[None])


MESH = pl.DeviceIdType.MESH
X, F, G = 0, 1, 2
STEP = 512
HALF_STEP = 256


def flip(index, bit):
    return index + bit - 2 * bit * lax.rem(lax.div(index, bit), 2)


def make_plan(route_row, own_expert, capacity):
    count = route_row.shape[1]
    row = route_row.astype(jnp.float32)
    at_row = lax.broadcasted_iota(jnp.int32, (count, count), 0)
    at_col = lax.broadcasted_iota(jnp.int32, (count, count), 1)
    wide = jnp.broadcast_to(row, (count, count))
    col = jnp.sum(jnp.where(at_row == at_col, wide, 0.0), axis=1, keepdims=True)
    same = jnp.where(wide == col, 1.0, 0.0)
    slot_col = jnp.sum(jnp.where(at_col < at_row, same, 0.0), axis=1, keepdims=True)
    slot_row = jnp.sum(jnp.where(at_row < at_col, same, 0.0), axis=0, keepdims=True)
    own = own_expert.astype(jnp.float32)

    def onehot(shape, axis, route, slot):
        at = lax.broadcasted_iota(jnp.int32, shape, axis).astype(jnp.float32)
        first = at < capacity
        expert = jnp.where(first, own, 1.0 - own)
        place = jnp.where(first, at, at - capacity)
        hit = jnp.where(route == expert, 1.0, 0.0) * jnp.where(slot == place, 1.0, 0.0)
        return hit.astype(jnp.bfloat16)

    pick = onehot((2 * capacity, count), 0, row, slot_row)
    spread = onehot((count, 2 * capacity), 1, col, slot_col)
    return pick, spread


def as_column(row):
    count = row.shape[1]
    at_row = lax.broadcasted_iota(jnp.int32, (count, count), 0)
    at_col = lax.broadcasted_iota(jnp.int32, (count, count), 1)
    wide = jnp.broadcast_to(row, (count, count))
    return jnp.sum(jnp.where(at_row == at_col, wide, 0.0), axis=1, keepdims=True)


def as_row(col):
    count = col.shape[0]
    at_row = lax.broadcasted_iota(jnp.int32, (count, count), 0)
    at_col = lax.broadcasted_iota(jnp.int32, (count, count), 1)
    wide = jnp.broadcast_to(col, (count, count))
    return jnp.sum(jnp.where(at_row == at_col, wide, 0.0), axis=0, keepdims=True)


def dot(a, b):
    return jnp.dot(a, b, preferred_element_type=jnp.float32)


def dot_t(a, b):
    return lax.dot_general(a, b, (((1,), (1,)), ((), ())), preferred_element_type=jnp.float32)


def layer_kernel(
    capacity,
    fa, fr, fw, ba, bg, br, bw, wg_hbm, wu_hbm, wd_hbm,
    mixed, in_grad, gate_grad,
    xf, xg, fold_s, fold_r, rows, wgu, wd, pre_x, pre_f, d_hid, hid, dd,
    part_f, part_x, core_f, core_x, two_f, two_x, one_f, one_x, last_s, last_r, own_s,
    w_sem, relay_s, relay_r, mir_s, mir_r, row_s, row_r, c_s, c_r, t_s, t_r, o_s, o_r, l_s, l_r,
):
    depth = fa.shape[1]
    half = depth // 2
    total = rows.shape[1] * rows.shape[2]
    unit = wd.shape[0]
    cap = capacity
    section = lax.axis_index("section")
    me = lax.axis_index("expert")
    core = lax.rem(me, 2)
    j = lax.rem(me, 8)
    base = me - j
    across, along = flip(j, 4), flip(j, 2)
    p1 = (1 - core) * across + core * along
    p2 = (1 - core) * along + core * across
    p12 = flip(flip(j, 4), 2)
    other = flip(j, 1)

    def in_group(k):
        return (section, base + k)

    mirror = (section, flip(me, 8))
    relay = (1 - section, me)
    barrier = pltpu.get_barrier_semaphore()
    for target in (relay, mirror, in_group(p1), in_group(p2), in_group(other)):
        pl.semaphore_signal(barrier, inc=1, device_id=target, device_id_type=MESH)
    pl.semaphore_wait(barrier, 5)

    def remote(src, dst, send, recv, target):
        return pltpu.make_async_remote_copy(
            src_ref=src, dst_ref=dst, send_sem=send, recv_sem=recv,
            device_id=target, device_id_type=MESH,
        )

    sent = []

    def go(copy):
        copy.start()
        sent.append(copy)
        return copy

    relay_f = remote(fa, xf, relay_s.at[0], relay_r.at[0], relay)
    relay_g = remote(bg, xg, relay_s.at[1], relay_r.at[1], relay)
    relay_f.start()
    loads = [
        pltpu.make_async_copy(wg_hbm, wgu.at[:, pl.ds(0, unit)], w_sem.at[0]),
        pltpu.make_async_copy(wu_hbm, wgu.at[:, pl.ds(unit, unit)], w_sem.at[1]),
        pltpu.make_async_copy(wd_hbm, wd, w_sem.at[2]),
    ]
    for load in loads:
        load.start()
    own_expert = lax.div(me, 8)
    pick_b, spread_b = make_plan(br[...], own_expert, cap)
    pick_f, spread_f = make_plan(fr[...], own_expert, cap)
    picks = (pick_b, pick_f, pick_b)
    sources = (ba, xf, xg)

    def halves(k):
        lo = pl.ds(pl.multiple_of(k * HALF_STEP, HALF_STEP), HALF_STEP)
        hi = pl.ds(pl.multiple_of(half + k * HALF_STEP, HALF_STEP), HALF_STEP)
        return lo, hi

    def mirror_copy(t):
        return remote(fold_s.at[t], fold_r.at[t], mir_s.at[t], mir_r.at[t], mirror)

    def pack(t):
        @pl.loop(0, half // HALF_STEP)
        def _(k):
            lo, hi = halves(k)
            away = picks[t][cap:]
            left, right = dot(away, sources[t][:, lo]), dot(away, sources[t][:, hi])
            fold_s[t, :, lo] = jnp.concatenate([left, right], axis=0).astype(jnp.bfloat16)

        go(mirror_copy(t))

    def row_copy(t, slot, send_at, target):
        block = rows.at[t, slot]
        return remote(block, block, row_s.at[t, send_at], row_r.at[t, slot], in_group(target))

    def form(t):
        mirror_copy(t).wait_recv()

        @pl.loop(0, half // HALF_STEP)
        def _(k):
            lo, hi = halves(k)
            near = picks[t][:cap]
            left, right = dot(near, sources[t][:, lo]), dot(near, sources[t][:, hi])
            got = fold_r[t, :, lo].astype(jnp.float32)
            rows[t, j, :, lo] = jnp.concatenate([left, got[:cap]], axis=0).astype(jnp.bfloat16)
            rows[t, j, :, hi] = jnp.concatenate([right, got[cap:]], axis=0).astype(jnp.bfloat16)

        go(row_copy(t, j, 0, p1))
        go(row_copy(t, j, 1, p2))
        go(row_copy(t, j, 2, other))

    def forward_first(t):
        row_copy(t, p1, 3, p2).wait_recv()
        go(row_copy(t, p1, 3, p2))
        go(row_copy(t, p1, 4, other))

    def forward_second(t):
        row_copy(t, p2, 5, other).wait_recv()
        go(row_copy(t, p2, 5, other))
        row_copy(t, p12, 6, other).wait_recv()
        go(row_copy(t, p12, 6, other))

    def gathered(t):
        for k in range(4):
            row_copy(t, 2 * k + 1 - core, 0, other).wait_recv()

    def columns(k):
        return pl.ds(pl.multiple_of(k * STEP, STEP), STEP)

    def gate_up(t, out):
        out[...] = jnp.zeros_like(out)

        @pl.loop(0, depth // STEP)
        def _(k):
            cols = columns(k)
            out[...] += dot(rows[t, :, :, cols].reshape(total, STEP), wgu[cols, :])

    def core_copy(o, k):
        part, box = ((part_f, core_f), (part_x, core_x))[o]
        return remote(
            part.at[2 * k + 1 - core], box.at[k], c_s.at[o, k], c_r.at[o, k], in_group(other)
        )

    def two_copy(o, k):
        part, box = ((part_f, two_f), (part_x, two_x))[o]
        return remote(
            part.at[(p2, p12)[k]], box.at[k], t_s.at[o, k], t_r.at[o, k], in_group(p2)
        )

    def one_copy(o):
        part, box = ((part_f, one_f), (part_x, one_x))[o]
        return remote(part.at[p1], box, o_s.at[o], o_r.at[o], in_group(p1))

    def last_copy(o):
        return remote(last_s.at[o], last_r.at[o], l_s.at[o], l_r.at[o], mirror)

    def add_into(ref, slot, box):
        ref[slot] = (
            ref[slot].astype(jnp.float32) + box.astype(jnp.float32)
        ).astype(jnp.bfloat16)

    def merge_core(o):
        part, box = ((part_f, core_f), (part_x, core_x))[o]
        for k in range(4):
            core_copy(o, k).wait_recv()

        @pl.loop(0, 4)
        def _(k):
            add_into(part, 2 * k + core, box[k])

        go(two_copy(o, 0))
        go(two_copy(o, 1))

    def merge_two(o):
        part, box = ((part_f, two_f), (part_x, two_x))[o]
        two_copy(o, 1).wait_recv()
        add_into(part, p1, box[1])
        go(one_copy(o))
        two_copy(o, 0).wait_recv()
        add_into(part, j, box[0])

    def merge_one(o):
        part, box = ((part_f, one_f), (part_x, one_x))[o]
        one_copy(o).wait_recv()

        def both(cols):
            return part[j, :, cols].astype(jnp.float32) + box[:, cols].astype(jnp.float32)

        @pl.loop(0, half // HALF_STEP)
        def _(k):
            lo, hi = halves(k)
            left, right = both(lo), both(hi)
            own_s[o, :, lo] = left[:cap]
            own_s[o, :, hi] = right[:cap]
            last_s[o, :, lo] = jnp.concatenate([left[cap:], right[cap:]], axis=0).astype(
                jnp.bfloat16
            )

        if o == 1:
            tail = both(pl.ds(depth, 128))
            own_s[o, :, pl.ds(depth, 128)] = tail[:cap]
            last_s[o, :, pl.ds(half, 128)] = jnp.concatenate(
                [tail[cap:], tail[cap:]], axis=0
            ).astype(jnp.bfloat16)
        else:
            last_s[o, :, pl.ds(half, 128)] = jnp.zeros((2 * cap, 128), jnp.bfloat16)
        go(last_copy(o))

    def finish(o, spread, weight_row, base_rows, out):
        last_copy(o).wait_recv()
        weight = as_column(weight_row)

        def spread_sum(near, far):
            return dot(spread, jnp.concatenate([near, far], axis=0).astype(jnp.bfloat16))

        @pl.loop(0, half // HALF_STEP)
        def _(k):
            lo, hi = halves(k)
            got = last_r[o, :, lo].astype(jnp.float32)
            for cols, far in ((lo, got[:cap]), (hi, got[cap:])):
                value = spread_sum(own_s[o, :, cols], far)
                out[:, cols] = (
                    base_rows[:, cols].astype(jnp.float32) + weight * value
                ).astype(jnp.bfloat16)

        if o == 1:
            far = last_r[o, :, pl.ds(half, 128)].astype(jnp.float32)[:cap]
            value = spread_sum(own_s[o, :, pl.ds(depth, 128)], far)
            gate_grad[...] = as_row(value[:, :1])

    pack(X)
    relay_f.wait_send()
    relay_g.start()
    form(X)
    relay_f.wait_recv()
    pack(F)
    forward_first(X)
    form(F)
    forward_second(X)
    relay_g.wait_recv()
    pack(G)
    forward_first(F)
    for load in loads:
        load.wait()
    gathered(X)
    gate_up(X, pre_x)
    form(G)
    forward_second(F)
    forward_first(G)
    gathered(F)
    gate_up(F, pre_f)
    gate = pre_f[:, :unit]
    hid[...] = (gate * jax.nn.sigmoid(gate) * pre_f[:, unit:]).astype(jnp.bfloat16)

    @pl.loop(0, depth // STEP)
    def _(k):
        cols = columns(k)
        part_f[:, :, cols] = (
            dot(hid[...], wd[:, cols]).astype(jnp.bfloat16).reshape(8, 2 * cap, STEP)
        )

    for k in range(4):
        go(core_copy(0, k))
    forward_second(G)
    merge_core(0)
    gathered(G)
    d_hid[...] = jnp.zeros_like(d_hid)

    @pl.loop(0, depth // STEP)
    def _(k):
        cols = columns(k)
        d_hid[...] += dot_t(rows[G, :, :, cols].reshape(total, STEP), wd[:, cols])

    gate = pre_x[:, :unit]
    up = pre_x[:, unit:]
    sig = jax.nn.sigmoid(gate)
    active = gate * sig
    hidden = (active * up).astype(jnp.bfloat16).astype(jnp.float32)
    grad = d_hid[...]
    dd[:, :unit] = (grad * up * sig * (1.0 + gate * (1.0 - sig))).astype(jnp.bfloat16)
    dd[:, unit:] = (grad * active).astype(jnp.bfloat16)
    term = jnp.sum(hidden * grad, axis=1, keepdims=True)
    part_x[:, :, pl.ds(depth, 128)] = (
        jnp.broadcast_to(term, (total, 128)).astype(jnp.bfloat16).reshape(8, 2 * cap, 128)
    )

    @pl.loop(0, depth // STEP)
    def _(k):
        cols = columns(k)
        part_x[:, :, cols] = (
            dot_t(dd[...], wgu[cols, :]).astype(jnp.bfloat16).reshape(8, 2 * cap, STEP)
        )

    for k in range(4):
        go(core_copy(1, k))
    merge_two(0)
    merge_core(1)
    merge_one(0)
    merge_two(1)
    finish(0, spread_f, fw[...], xf, mixed)
    merge_one(1)
    finish(1, spread_b, bw[...], xg, in_grad)
    relay_g.wait_send()
    for copy in sent:
        copy.wait_send()


def local_tree(
    fwd_act, fwd_route, fwd_weight, bwd_act, bwd_grad, bwd_route, bwd_weight, w_gate, w_up, w_down
):
    count, depth = fwd_act.shape[1:]
    unit = w_gate.shape[2]
    cap = 3 * count // 8
    pair = 2 * cap
    wide = depth + 128
    half = depth // 2
    bf16, f32 = jnp.bfloat16, jnp.float32
    vmem = pl.BlockSpec(memory_space=pltpu.VMEM)
    hbm = pl.BlockSpec(memory_space=pl.ANY)
    dma = pltpu.SemaphoreType.DMA
    buf = pltpu.VMEM
    mixed, in_grad, gate_grad = pl.pallas_call(
        functools.partial(layer_kernel, cap),
        out_shape=(
            jax.ShapeDtypeStruct((count, depth), bf16),
            jax.ShapeDtypeStruct((count, depth), bf16),
            jax.ShapeDtypeStruct((1, count), f32),
        ),
        in_specs=[vmem] * 7 + [hbm] * 3,
        out_specs=(vmem, vmem, vmem),
        scratch_shapes=[
            buf((count, depth), bf16),
            buf((count, depth), bf16),
            buf((3, pair, half), bf16),
            buf((3, pair, half), bf16),
            buf((3, 8, pair, depth), bf16),
            buf((depth, 2 * unit), bf16),
            buf((unit, depth), bf16),
            buf((8 * pair, 2 * unit), f32),
            buf((8 * pair, 2 * unit), f32),
            buf((8 * pair, unit), f32),
            buf((8 * pair, unit), bf16),
            buf((8 * pair, 2 * unit), bf16),
            buf((8, pair, depth), bf16),
            buf((8, pair, wide), bf16),
            buf((4, pair, depth), bf16),
            buf((4, pair, wide), bf16),
            buf((2, pair, depth), bf16),
            buf((2, pair, wide), bf16),
            buf((pair, depth), bf16),
            buf((pair, wide), bf16),
            buf((2, pair, half + 128), bf16),
            buf((2, pair, half + 128), bf16),
            buf((2, cap, wide), f32),
            dma((3,)), dma((2,)), dma((2,)), dma((3,)), dma((3,)),
            dma((3, 7)), dma((3, 8)), dma((2, 4)), dma((2, 4)), dma((2, 2)), dma((2, 2)),
            dma((2,)), dma((2,)), dma((2,)), dma((2,)),
        ],
        compiler_params=pltpu.CompilerParams(
            collective_id=0, has_side_effects=True, vmem_limit_bytes=50 * 1024 * 1024
        ),
        cost_estimate=pl.CostEstimate(
            flops=2 * 8 * 8 * pair * depth * unit, bytes_accessed=6_000_000, transcendentals=100_000
        ),
    )(
        fwd_act[0], fwd_route, fwd_weight, bwd_act[0], bwd_grad[0], bwd_route, bwd_weight,
        w_gate[0], w_up[0], w_down[0],
    )
    return (mixed[None], in_grad[None], gate_grad)


def solution(mesh):
    placed = (
        P("section", "expert", None),
        P("section", "expert"),
        P("section", "expert"),
        P("section", "expert", None),
        P("section", "expert", None),
        P("section", "expert"),
        P("section", "expert"),
        P("section", None, "expert"),
        P("section", None, "expert"),
        P("section", "expert", None),
    )
    pair_of_experts = mesh.shape["section"] == 2 and mesh.shape["expert"] == 16
    return jax.shard_map(
        local_tree if pair_of_experts else local,
        mesh=mesh,
        in_specs=placed,
        out_specs=(
            P("section", "expert", None),
            P("section", "expert", None),
            P("section", "expert"),
        ),
        check_vma=False,
    )
```

```python
import functools

import jax
import jax.numpy as jnp
from jax import lax
from jax.experimental import pallas as pl
from jax.experimental.pallas import tpu as pltpu
from jax.sharding import PartitionSpec as P

FF = 1024


def passed_along(block, axis, distance):
    devices = range(lax.axis_size(axis))
    route = [((i - distance) % len(devices), i) for i in devices]
    return lax.ppermute(block, axis, route)


def route_plan(route_ids, experts, capacity):
    route_range = jnp.arange(2 * experts, dtype=jnp.int32)
    onehot = (route_ids[:, None] == route_range[None, :]).astype(jnp.int32)
    before = jnp.cumsum(onehot, axis=0) - onehot
    slot_ids = jnp.sum(before * onehot, axis=1)
    inside = route_ids < experts
    expert_ids = jnp.arange(experts, dtype=jnp.int32)
    slot_range = jnp.arange(capacity, dtype=jnp.int32)
    select = (
        (route_ids[None, None, :] == expert_ids[:, None, None])
        & (slot_ids[None, None, :] == slot_range[None, :, None])
    ).astype(jnp.bfloat16)
    place_at = jnp.where(inside, route_ids * capacity + slot_ids, 0)
    return (select, place_at, inside)


def pack_rows(select, token_rows, group_size):
    packed = jnp.einsum(
        "ect,td->ecd", select, token_rows, preferred_element_type=jnp.float32
    ).astype(jnp.bfloat16)
    copies = jnp.broadcast_to(packed[:, None], (packed.shape[0], group_size) + packed.shape[1:])
    return copies.reshape((packed.shape[0] * group_size,) + packed.shape[1:])


def unpack_sum(returned, group_size, place_at, inside):
    grouped = returned.astype(jnp.float32).reshape(
        (returned.shape[0] // group_size, group_size) + returned.shape[1:]
    )
    summed = jnp.sum(grouped, axis=1)
    flat = summed.reshape((summed.shape[0] * summed.shape[1],) + summed.shape[2:])
    picked = flat[place_at]
    mask = inside.reshape(inside.shape + (1,) * (picked.ndim - 1))
    return jnp.where(mask, picked, 0.0)


def expert_forward(token_rows, gate_cols, up_cols, down_rows):
    gate_pre = jnp.einsum("scd,dh->sch", token_rows, gate_cols, preferred_element_type=jnp.float32)
    up_pre = jnp.einsum("scd,dh->sch", token_rows, up_cols, preferred_element_type=jnp.float32)
    hidden = (jax.nn.silu(gate_pre) * up_pre).astype(jnp.bfloat16)
    return jnp.einsum("sch,hd->scd", hidden, down_rows, preferred_element_type=jnp.float32).astype(
        jnp.bfloat16
    )


def expert_backward(token_rows, grad_rows, gate_cols, up_cols, down_rows):
    gate_pre = jnp.einsum("scd,dh->sch", token_rows, gate_cols, preferred_element_type=jnp.float32)
    up_pre = jnp.einsum("scd,dh->sch", token_rows, up_cols, preferred_element_type=jnp.float32)
    gate_sig = jax.nn.sigmoid(gate_pre)
    active = gate_pre * gate_sig
    hidden = (active * up_pre).astype(jnp.bfloat16)
    d_hidden = jnp.einsum("scd,hd->sch", grad_rows, down_rows, preferred_element_type=jnp.float32)
    d_gate = (d_hidden * up_pre * gate_sig * (1.0 + gate_pre * (1.0 - gate_sig))).astype(
        jnp.bfloat16
    )
    d_up = (d_hidden * active).astype(jnp.bfloat16)
    d_rows = jnp.einsum("sch,dh->scd", d_gate, gate_cols, preferred_element_type=jnp.float32)
    d_rows = (
        d_rows + jnp.einsum("sch,dh->scd", d_up, up_cols, preferred_element_type=jnp.float32)
    ).astype(jnp.bfloat16)
    terms = jnp.sum(hidden.astype(jnp.float32) * d_hidden, axis=2).astype(jnp.bfloat16)
    return (d_rows, terms)


def local(
    fwd_act, fwd_route, fwd_weight, bwd_act, bwd_grad, bwd_route, bwd_weight, w_gate, w_up, w_down
):
    layer_in = passed_along(fwd_act, "section", 1)[0]
    grad_in = passed_along(bwd_grad, "section", -1)[0]
    gate_cols = w_gate[0]
    up_cols = w_up[0]
    down_rows = w_down[0]
    group_size = FF // gate_cols.shape[1]
    experts = lax.axis_size("expert") // group_size
    tok_count = layer_in.shape[0]
    capacity = 3 * tok_count // (4 * experts)
    select_f, place_f, inside_f = route_plan(fwd_route[0], experts, capacity)
    select_b, place_b, inside_b = route_plan(bwd_route[0], experts, capacity)
    sent_f = pack_rows(select_f, layer_in, group_size)
    sent_x = pack_rows(select_b, bwd_act[0], group_size)
    sent_g = pack_rows(select_b, grad_in, group_size)
    part_out = expert_forward(
        lax.all_to_all(sent_f, "expert", split_axis=0, concat_axis=0, tiled=True),
        gate_cols,
        up_cols,
        down_rows,
    )
    back_f = lax.all_to_all(part_out, "expert", split_axis=0, concat_axis=0, tiled=True)
    d_rows, terms = expert_backward(
        lax.all_to_all(sent_x, "expert", split_axis=0, concat_axis=0, tiled=True),
        lax.all_to_all(sent_g, "expert", split_axis=0, concat_axis=0, tiled=True),
        gate_cols,
        up_cols,
        down_rows,
    )
    back_x = lax.all_to_all(d_rows, "expert", split_axis=0, concat_axis=0, tiled=True)
    back_w = lax.all_to_all(terms, "expert", split_axis=0, concat_axis=0, tiled=True)
    total_f = unpack_sum(back_f, group_size, place_f, inside_f)
    total_x = unpack_sum(back_x, group_size, place_b, inside_b)
    gate_grad = unpack_sum(back_w, group_size, place_b, inside_b)
    mixed = (layer_in.astype(jnp.float32) + fwd_weight[0][:, None] * total_f).astype(jnp.bfloat16)
    input_grad = (grad_in.astype(jnp.float32) + bwd_weight[0][:, None] * total_x).astype(
        jnp.bfloat16
    )
    return (mixed[None], input_grad[None], gate_grad[None])


MESH = pl.DeviceIdType.MESH
X, F, G = 0, 1, 2
HALF_STEP = 256


def flip(index, bit):
    return index + bit - 2 * bit * lax.rem(lax.div(index, bit), 2)


def make_plan(route_row, own_expert, capacity):
    count = route_row.shape[1]
    row = route_row.astype(jnp.float32)
    at_row = lax.broadcasted_iota(jnp.int32, (count, count), 0)
    at_col = lax.broadcasted_iota(jnp.int32, (count, count), 1)
    wide = jnp.broadcast_to(row, (count, count))
    col = jnp.sum(jnp.where(at_row == at_col, wide, 0.0), axis=1, keepdims=True)
    same = jnp.where(wide == col, 1.0, 0.0)
    slot_col = jnp.sum(jnp.where(at_col < at_row, same, 0.0), axis=1, keepdims=True)
    slot_row = jnp.sum(jnp.where(at_row < at_col, same, 0.0), axis=0, keepdims=True)
    own = own_expert.astype(jnp.float32)

    def onehot(shape, axis, route, slot):
        at = lax.broadcasted_iota(jnp.int32, shape, axis).astype(jnp.float32)
        first = at < capacity
        expert = jnp.where(first, own, 1.0 - own)
        place = jnp.where(first, at, at - capacity)
        hit = jnp.where(route == expert, 1.0, 0.0) * jnp.where(slot == place, 1.0, 0.0)
        return hit.astype(jnp.bfloat16)

    pick = onehot((2 * capacity, count), 0, row, slot_row)
    spread = onehot((count, 2 * capacity), 1, col, slot_col)
    return pick, spread


def as_column(row):
    count = row.shape[1]
    at_row = lax.broadcasted_iota(jnp.int32, (count, count), 0)
    at_col = lax.broadcasted_iota(jnp.int32, (count, count), 1)
    wide = jnp.broadcast_to(row, (count, count))
    return jnp.sum(jnp.where(at_row == at_col, wide, 0.0), axis=1, keepdims=True)


def as_row(col):
    count = col.shape[0]
    at_row = lax.broadcasted_iota(jnp.int32, (count, count), 0)
    at_col = lax.broadcasted_iota(jnp.int32, (count, count), 1)
    wide = jnp.broadcast_to(col, (count, count))
    return jnp.sum(jnp.where(at_row == at_col, wide, 0.0), axis=0, keepdims=True)


def dot(a, b):
    return jnp.dot(a, b, preferred_element_type=jnp.float32)


def dot_t(a, b):
    return lax.dot_general(a, b, (((1,), (1,)), ((), ())), preferred_element_type=jnp.float32)


def layer_kernel(
    capacity,
    fa, fr_hbm, fw_hbm, ba_hbm, bg, br_hbm, bw_hbm, wg_hbm, wu_hbm, wd_hbm,
    mixed, in_grad, gate_grad,
    fr, fw, br, bw, xb, xf, xg, fold_s, rows, wgu, wd, pre_x, pre_f, hid, dd,
    part_f, part_x, core_f, core_x, two_f, two_x, one_f, one_x, last_s, last_r, own_s,
    w_sem, relay_s, relay_r, mir_s, mir_r, row_s, row_r, c_s, c_r, t_s, t_r, o_s, o_r, l_s, l_r,
):
    depth = xb.shape[1]
    half = depth // 2
    unit = wd.shape[0] // 2
    cap = capacity
    section = lax.axis_index("section")
    me = lax.axis_index("expert")
    core = lax.rem(me, 2)
    j = lax.rem(me, 8)
    base = me - j
    across, along = flip(j, 4), flip(j, 2)
    first = (across, (1 - core) * across + core * along)
    second = (along, (1 - core) * along + core * across)
    corner = flip(across, 2)
    other = flip(j, 1)

    def in_group(k):
        return (section, base + k)

    mirror = (section, flip(me, 8))
    relay = (1 - section, me)
    loads = [
        pltpu.make_async_copy(src, dst, w_sem.at[k])
        for k, (src, dst) in enumerate(
            (
                (ba_hbm, xb),
                (br_hbm, br),
                (fr_hbm, fr),
                (bw_hbm, bw),
                (fw_hbm, fw),
                (wg_hbm.at[pl.ds(0, half)], wgu.at[:, pl.ds(0, unit)]),
                (wu_hbm.at[pl.ds(0, half)], wgu.at[:, pl.ds(unit, unit)]),
                (wg_hbm.at[pl.ds(half, half)], wgu.at[:, pl.ds(2 * unit, unit)]),
                (wu_hbm.at[pl.ds(half, half)], wgu.at[:, pl.ds(3 * unit, unit)]),
                (wd_hbm.at[:, pl.ds(0, half)], wd.at[pl.ds(0, unit)]),
                (wd_hbm.at[:, pl.ds(half, half)], wd.at[pl.ds(unit, unit)]),
            )
        )
    ]
    for load in loads:
        load.start()
    barrier = pltpu.get_barrier_semaphore()
    for target in (relay, mirror, in_group(across), in_group(along), in_group(other)):
        pl.semaphore_signal(barrier, inc=1, device_id=target, device_id_type=MESH)
    pl.semaphore_wait(barrier, 5)

    def remote(src, dst, send, recv, target):
        return pltpu.make_async_remote_copy(
            src_ref=src, dst_ref=dst, send_sem=send, recv_sem=recv,
            device_id=target, device_id_type=MESH,
        )

    sent = []

    def go(copy):
        copy.start()
        sent.append(copy)

    relay_f = remote(fa, xf, relay_s.at[0], relay_r.at[0], relay)
    relay_g = remote(bg, xg, relay_s.at[1], relay_r.at[1], relay)
    relay_f.start()
    for load in loads[:5]:
        load.wait()
    own_expert = lax.div(me, 8)
    pick_b, spread_b = make_plan(br[...], own_expert, cap)
    pick_f, spread_f = make_plan(fr[...], own_expert, cap)
    picks = (pick_b, pick_f, pick_b)
    sources = (xb, xf, xg)

    def halves(k):
        lo = pl.ds(pl.multiple_of(k * HALF_STEP, HALF_STEP), HALF_STEP)
        hi = pl.ds(pl.multiple_of(half + k * HALF_STEP, HALF_STEP), HALF_STEP)
        return lo, hi

    def mirror_copy(t):
        return remote(fold_s.at[t], rows.at[t, 1, j], mir_s.at[t], mir_r.at[t], mirror)

    def row_copy(t, m, slot, send_at, target):
        block = rows.at[t, m, slot]
        return remote(
            block, block, row_s.at[t, m, send_at], row_r.at[t, m, slot], in_group(target)
        )

    def send_block(t, m):
        go(row_copy(t, m, j, 0, first[m]))
        go(row_copy(t, m, j, 1, second[m]))
        go(row_copy(t, m, j, 2, other))

    def pack(t):
        @pl.loop(0, half // HALF_STEP)
        def _(k):
            lo, hi = halves(k)
            left, right = dot(picks[t], sources[t][:, lo]), dot(picks[t], sources[t][:, hi])
            fold_s[t, :, lo] = jnp.concatenate([left[cap:], right[cap:]], axis=0).astype(
                jnp.bfloat16
            )
            rows[t, 0, j, :, lo] = jnp.concatenate([left[:cap], right[:cap]], axis=0).astype(
                jnp.bfloat16
            )

        go(mirror_copy(t))
        send_block(t, 0)

    def mirror_in(t):
        mirror_copy(t).wait_recv()
        send_block(t, 1)

    def forward_first(t, m):
        row_copy(t, m, first[m], 3, second[m]).wait_recv()
        go(row_copy(t, m, first[m], 3, second[m]))
        go(row_copy(t, m, first[m], 4, other))

    def forward_second(t, m):
        for slot, at in ((second[m], 5), (corner, 6)):
            row_copy(t, m, slot, at, other).wait_recv()
            go(row_copy(t, m, slot, at, other))

    def gathered(t, m):
        for k in range(4):
            row_copy(t, m, 2 * k + 1 - core, 0, other).wait_recv()

    def unfold(value, width):
        blocks = value.reshape(8, 2 * cap, 2 * width)
        return (blocks[:, :cap, :width] + blocks[:, cap:, width:]).reshape(8 * cap, width)

    def gate_up(t, m, out):
        gathered(t, m)
        out[m] = unfold(dot(rows[t, m].reshape(16 * cap, half), wgu[...]), 2 * unit)

    def fold(left, right):
        width = left.shape[1]
        both = [left.reshape(8, cap, width), right.reshape(8, cap, width)]
        return jnp.concatenate(both, axis=1).astype(jnp.bfloat16)

    def forward_out(m):
        gate = pre_f[m, :, :unit]
        up = pre_f[m, :, unit:]
        hid[m] = (gate * jax.nn.sigmoid(gate) * up).astype(jnp.bfloat16)

        @pl.loop(0, half // HALF_STEP)
        def _(k):
            lo, _ = halves(k)
            part_f[m, :, :, lo] = fold(dot(hid[m], wd[:unit, lo]), dot(hid[m], wd[unit:, lo]))

        send_core(0, m)

    def backward_out(m):
        gathered(G, m)
        grad = unfold(dot_t(rows[G, m].reshape(16 * cap, half), wd[...]), unit)
        gate = pre_x[m, :, :unit]
        up = pre_x[m, :, unit:]
        sig = jax.nn.sigmoid(gate)
        active = gate * sig
        hidden = (active * up).astype(jnp.bfloat16).astype(jnp.float32)
        dd[m, :, :unit] = (grad * up * sig * (1.0 + gate * (1.0 - sig))).astype(jnp.bfloat16)
        dd[m, :, unit:] = (grad * active).astype(jnp.bfloat16)
        term = jnp.broadcast_to(jnp.sum(hidden * grad, axis=1, keepdims=True), (8 * cap, 128))
        part_x[m, :, :, pl.ds(half, 128)] = fold(term, term)

        @pl.loop(0, half // HALF_STEP)
        def _(k):
            lo, _ = halves(k)
            part_x[m, :, :, lo] = fold(
                dot_t(dd[m], wgu[lo, : 2 * unit]), dot_t(dd[m], wgu[lo, 2 * unit :])
            )

        send_core(1, m)

    parts, cores = (part_f, part_x), (core_f, core_x)
    twos, ones = (two_f, two_x), (one_f, one_x)

    def core_copy(o, m, k):
        return remote(
            parts[o].at[m, 2 * k + 1 - core], cores[o].at[m, k],
            c_s.at[o, m, k], c_r.at[o, m, k], in_group(other),
        )

    def two_copy(o, m, k):
        return remote(
            parts[o].at[m, (second[m], corner)[k]], twos[o].at[m, k],
            t_s.at[o, m, k], t_r.at[o, m, k], in_group(second[m]),
        )

    def one_copy(o, m):
        return remote(
            parts[o].at[m, first[m]], ones[o].at[m], o_s.at[o, m], o_r.at[o, m],
            in_group(first[m]),
        )

    def last_copy(o):
        return remote(last_s.at[o], last_r.at[o], l_s.at[o], l_r.at[o], mirror)

    def send_core(o, m):
        for k in range(4):
            go(core_copy(o, m, k))

    def add_into(ref, m, slot, box):
        ref[m, slot] = (
            ref[m, slot].astype(jnp.float32) + box.astype(jnp.float32)
        ).astype(jnp.bfloat16)

    def merge_core(o, m):
        for k in range(4):
            core_copy(o, m, k).wait_recv()

        @pl.loop(0, 4)
        def _(k):
            add_into(parts[o], m, 2 * k + core, cores[o][m, k])

        go(two_copy(o, m, 1))
        go(two_copy(o, m, 0))

    def merge_two(o, m):
        two_copy(o, m, 1).wait_recv()
        add_into(parts[o], m, first[m], twos[o][m, 1])
        go(one_copy(o, m))
        two_copy(o, m, 0).wait_recv()
        add_into(parts[o], m, j, twos[o][m, 0])

    def merge_one(o, m):
        one_copy(o, m).wait_recv()
        width = parts[o].shape[-1]
        value = parts[o][m, j].astype(jnp.float32) + ones[o][m].astype(jnp.float32)
        target = (own_s, last_s)[m]
        target[o, :, :width] = value.astype(jnp.bfloat16)
        if width < target.shape[-1]:
            rest = (value.shape[0], target.shape[-1] - width)
            target[o, :, width:] = jnp.zeros(rest, jnp.bfloat16)
        if m == 1:
            go(last_copy(o))

    def finish(o, spread, weight_row, base_rows, out):
        last_copy(o).wait_recv()
        weight = as_column(weight_row)

        def spread_sums(cols):
            near = own_s[o, :, cols].astype(jnp.float32)
            far = last_r[o, :, cols].astype(jnp.float32)
            left = jnp.concatenate([near[:cap], far[:cap]], axis=0).astype(jnp.bfloat16)
            right = jnp.concatenate([near[cap:], far[cap:]], axis=0).astype(jnp.bfloat16)
            return dot(spread, left), dot(spread, right)

        @pl.loop(0, half // HALF_STEP)
        def _(k):
            lo, hi = halves(k)
            for cols, value in zip((lo, hi), spread_sums(lo)):
                out[:, cols] = (
                    base_rows[:, cols].astype(jnp.float32) + weight * value
                ).astype(jnp.bfloat16)

        if o == 1:
            value, _ = spread_sums(pl.ds(half, 128))
            gate_grad[...] = as_row(value[:, :1])

    pack(X)
    forward_first(X, 0)
    mirror_in(X)
    relay_f.wait_recv()
    relay_f.wait_send()
    relay_g.start()
    pack(F)
    forward_first(X, 1)
    forward_second(X, 0)
    mirror_in(F)
    forward_first(F, 0)
    forward_second(X, 1)
    for load in loads[5:]:
        load.wait()
    gate_up(X, 0, pre_x)
    relay_g.wait_recv()
    pack(G)
    forward_first(F, 1)
    forward_second(F, 0)
    gate_up(X, 1, pre_x)
    mirror_in(G)
    forward_first(G, 0)
    forward_second(F, 1)
    gate_up(F, 0, pre_f)
    gate_up(F, 1, pre_f)
    forward_out(1)
    forward_first(G, 1)
    forward_out(0)
    forward_second(G, 0)
    merge_core(0, 1)
    merge_core(0, 0)
    forward_second(G, 1)
    backward_out(1)
    backward_out(0)
    merge_two(0, 1)
    merge_core(1, 1)
    merge_core(1, 0)
    merge_two(0, 0)
    merge_one(0, 1)
    merge_two(1, 1)
    merge_one(0, 0)
    merge_two(1, 0)
    merge_one(1, 1)
    finish(0, spread_f, fw[...], xf, mixed)
    merge_one(1, 0)
    finish(1, spread_b, bw[...], xg, in_grad)
    relay_g.wait_send()
    for copy in sent:
        copy.wait_send()


def local_tree(
    fwd_act, fwd_route, fwd_weight, bwd_act, bwd_grad, bwd_route, bwd_weight, w_gate, w_up, w_down
):
    count, depth = fwd_act.shape[1:]
    unit = w_gate.shape[2]
    cap = 3 * count // 8
    pair = 2 * cap
    half = depth // 2
    wide = half + 128
    bf16, f32, i32 = jnp.bfloat16, jnp.float32, jnp.int32
    vmem = pl.BlockSpec(memory_space=pltpu.VMEM)
    hbm = pl.BlockSpec(memory_space=pl.ANY)
    dma = pltpu.SemaphoreType.DMA
    buf = pltpu.VMEM
    mixed, in_grad, gate_grad = pl.pallas_call(
        functools.partial(layer_kernel, cap),
        out_shape=(
            jax.ShapeDtypeStruct((count, depth), bf16),
            jax.ShapeDtypeStruct((count, depth), bf16),
            jax.ShapeDtypeStruct((1, count), f32),
        ),
        in_specs=[hbm] * 10,
        out_specs=(vmem, vmem, vmem),
        scratch_shapes=[
            buf((1, count), i32),
            buf((1, count), f32),
            buf((1, count), i32),
            buf((1, count), f32),
            buf((count, depth), bf16),
            buf((count, depth), bf16),
            buf((count, depth), bf16),
            buf((3, pair, half), bf16),
            buf((3, 2, 8, pair, half), bf16),
            buf((half, 4 * unit), bf16),
            buf((2 * unit, half), bf16),
            buf((2, 8 * cap, 2 * unit), f32),
            buf((2, 8 * cap, 2 * unit), f32),
            buf((2, 8 * cap, unit), bf16),
            buf((2, 8 * cap, 2 * unit), bf16),
            buf((2, 8, pair, half), bf16),
            buf((2, 8, pair, wide), bf16),
            buf((2, 4, pair, half), bf16),
            buf((2, 4, pair, wide), bf16),
            buf((2, 2, pair, half), bf16),
            buf((2, 2, pair, wide), bf16),
            buf((2, pair, half), bf16),
            buf((2, pair, wide), bf16),
            buf((2, pair, wide), bf16),
            buf((2, pair, wide), bf16),
            buf((2, pair, wide), bf16),
            dma((11,)), dma((2,)), dma((2,)), dma((3,)), dma((3,)),
            dma((3, 2, 7)), dma((3, 2, 8)), dma((2, 2, 4)), dma((2, 2, 4)),
            dma((2, 2, 2)), dma((2, 2, 2)), dma((2, 2)), dma((2, 2)), dma((2,)), dma((2,)),
        ],
        compiler_params=pltpu.CompilerParams(
            collective_id=0, has_side_effects=True, vmem_limit_bytes=58 * 1024 * 1024
        ),
        cost_estimate=pl.CostEstimate(
            flops=2 * 8 * 8 * pair * depth * unit, bytes_accessed=6_000_000, transcendentals=100_000
        ),
    )(
        fwd_act[0], fwd_route, fwd_weight, bwd_act[0], bwd_grad[0], bwd_route, bwd_weight,
        w_gate[0], w_up[0], w_down[0],
    )
    return (mixed[None], in_grad[None], gate_grad)


def solution(mesh):
    placed = (
        P("section", "expert", None),
        P("section", "expert"),
        P("section", "expert"),
        P("section", "expert", None),
        P("section", "expert", None),
        P("section", "expert"),
        P("section", "expert"),
        P("section", None, "expert"),
        P("section", None, "expert"),
        P("section", "expert", None),
    )
    pair_of_experts = mesh.shape["section"] == 2 and mesh.shape["expert"] == 16
    return jax.shard_map(
        local_tree if pair_of_experts else local,
        mesh=mesh,
        in_specs=placed,
        out_specs=(
            P("section", "expert", None),
            P("section", "expert", None),
            P("section", "expert"),
        ),
        check_vma=False,
    )
```
